32 devices in a mesh: parts: 2 (over x), rows: 16 (over z, y, core).
Axes of the slice: x: 2, y: 2, z: 4, core: 2. Of those that a mesh axis runs over, the one named last changes fastest.
Arguments:
- lap_tiles: float32 [512, 7, 128, 128], P(('parts', 'rows')), parts along dimension 0, may hold values from -91.799777 to 91.799777, as said below
- tile_columns: int32 [512, 7], P(('parts', 'rows')), parts along dimension 0, may hold values from 0 to 255, as said below
- start_block: float32 [65536, 64], P(('parts', 'rows')), parts along dimension 0, may hold values from -6 to 6
- patch_of: int32 [65536, 1], P(('parts', 'rows')), parts along dimension 0, may hold values from 0 to 63; in each aligned block of 2048 rows (0 to 2047, 2048 to 4095, ...) at most 64 rows name the same one
- mix_weight: bfloat16 [128, 256], replicated, may hold values from -0.5 to 0.5
- class_weight: bfloat16 [256, 16], replicated, may hold values from -0.375 to 0.375
Outputs:
- embedding: bfloat16 [65536, 64], P(('parts', 'rows')), parts along dimension 0
- ritz: float32 [128, 64], P('parts'), parts along dimension 0
- labels: bfloat16 [65536, 16], P(('parts', 'rows')), parts along dimension 0
The draws below stay inside these ranges and needn't reach their ends.
There are 2 independent parts, one for each index of `parts`. The reference program is written for one: setup_inputs(seed, part) draws one part's arguments, and reference() takes and returns one part's arrays. A program takes and returns all parts, laid end to end along the dimension named above; an argument that names none is the same for every part. Nothing has to cross between parts.
Inputs may be any that keep to these rules, and one draw needn't show every extreme that they name: L is symmetric: where tile_columns[b, t] = c, block c has a tile with column block b, and that tile is the transpose of lap_tiles[b, t]. Each vertex's row of L, over all tiles of its row block, sums to zero. `tile_columns`: tile 0 of row block b has column block b; the tiles of one row block name distinct column blocks, each among the device's own row blocks or within 2 row blocks beyond them on either side, counted cyclically over the 256 blocks. `patch_of`: among the 2048 vertices of one device no patch occurs more than 64 times; every patch has at least one vertex.
All inputs are finite; a program needn't handle non-finite values.
Results may differ from the reference program's by a relative error of at most 0.0058.
Values may be sent and summed in bfloat16 or wider, within the bound.
A program may use at most 64 MiB of HBM per device.

```python
import math
import jax
import jax.numpy as jnp
import numpy as np
from jax import lax

TILE = 128
K = 64
HID = 256
NCLS = 16
TPB = 7
RB = 16
V_DEV = 2048
NB = 256
V = 32768
PATCHES = 64
CAP = 64


def block_pattern(key):
    base = jax.random.fold_in(key, 101)
    blocks = jnp.arange(NB, dtype=jnp.int32)
    inner = [jnp.bitwise_xor(blocks, jnp.int32(m)) for m in (1, 2, 3)]
    moved = (blocks + 2) % NB
    across = [(jnp.bitwise_xor(moved, jnp.int32(m)) - 2) % NB for m in (2, 3)]
    masks = 4 * jax.random.randint(jax.random.fold_in(base, 1), (NB // RB,), 1, RB // 4, dtype=jnp.int32)
    distant = jnp.bitwise_xor(blocks, masks[blocks // RB])
    others = jnp.stack(inner + across + [distant], axis=1)
    scores = jax.random.randint(jax.random.fold_in(base, 2), (NB, 6), 0, 1 << 20, dtype=jnp.int32) * 8 + jnp.arange(6, dtype=jnp.int32)[None, :]
    order = jnp.argsort(scores, axis=1)
    others = jnp.take_along_axis(others, order, axis=1)
    return jnp.concatenate([blocks[:, None], others], axis=1).astype(jnp.int32)


def draw_tile_columns(key, part):
    return block_pattern(key)


def draw_lap_tiles(key, part):
    columns = block_pattern(key)
    key = jax.random.fold_in(key, 7)
    sigma = (4.0 * TPB * TILE) ** (-0.5)
    offset = 2.0 / (TPB * TILE)
    blocks = jnp.arange(NB, dtype=jnp.int32)
    row_ids = jnp.broadcast_to(blocks[:, None], (NB, 6))
    col_ids = columns[:, 1:]
    low = jnp.minimum(row_ids, col_ids)
    high = jnp.maximum(row_ids, col_ids)
    pair_ids = (low * NB + high).reshape(-1)
    pair_key = jax.random.fold_in(key, 1)

    def one_pair(ident):
        return jnp.clip(jax.random.normal(jax.random.fold_in(pair_key, ident), (TILE, TILE), jnp.float32), -6.0, 6.0)
    raw = jax.vmap(one_pair)(pair_ids).reshape(NB, 6, TILE, TILE)
    weights = sigma * raw + offset
    flip = (row_ids > col_ids)[:, :, None, None]
    weights = jnp.where(flip, jnp.swapaxes(weights, -1, -2), weights)
    own_key = jax.random.fold_in(key, 2)

    def one_block(ident):
        return jnp.clip(jax.random.normal(jax.random.fold_in(own_key, ident), (TILE, TILE), jnp.float32), -6.0, 6.0)
    own = jax.vmap(one_block)(blocks)
    outside = 1.0 - jnp.eye(TILE, dtype=jnp.float32)
    own_weights = (sigma * 0.5 * (own + jnp.swapaxes(own, -1, -2)) + offset) * outside[None]
    degree = jnp.sum(weights, axis=(1, 3)) + jnp.sum(own_weights, axis=2)
    first = degree[:, :, None] * jnp.eye(TILE, dtype=jnp.float32)[None] - own_weights
    return jnp.concatenate([first[:, None], -weights], axis=1).astype(jnp.float32)


def shard_levels(rng, dims, shards, least, largest):
    def one(axis_at, parts):
        heights = jax.random.uniform(jax.random.fold_in(jax.random.fold_in(rng, 6), axis_at), (parts,), jnp.float32, least / len(shards), largest / len(shards))
        return jnp.repeat(jnp.exp(heights), dims[axis_at] // parts).reshape((-1,) + (1,) * (len(dims) - axis_at - 1))

    gain = one(*shards[0])
    for cut in shards[1:]:
        gain = gain * one(*cut)
    return gain


def assign_block(rng, own, number, rows, number_of, top, limit, skew):
    order = jax.random.permutation(rng, number_of)
    heavy_load, ordinary = portions_of(number_of, rows * top, limit, skew, True), portions_of(number_of, rows * top, limit, skew, False)
    places = jnp.arange(number_of)

    def named(tallies, turn):
        used = int((tallies > 0).sum())
        fixed = max(1, used // 4)
        passed = fixed + (places - fixed + turn * (used - fixed)) % max(1, number_of - fixed)
        return jnp.zeros((number_of,), jnp.int32).at[order[jnp.where(places < fixed, places, passed)]].set(jnp.asarray(tallies, jnp.int32))

    tallies = jnp.where(number % 4 == 0, named(heavy_load, number // 4), named(ordinary, number - number // 4 - 1))
    mixed = jax.random.permutation(jax.random.fold_in(own, 3), number_of)
    source_of, sink = mixed[0:number_of // 2 * 2:2], mixed[1:number_of // 2 * 2:2]
    margin = jnp.minimum(tallies[source_of] - 1, limit - tallies[sink]) // 2
    margin = jnp.where((source_of == order[0]) | (sink == order[0]) | (tallies[sink] == 0), 0, jnp.maximum(margin, 0))
    passed = jax.random.randint(jax.random.fold_in(own, 4), (number_of // 2,), 0, 1 << 20) % (margin + 1)
    tallies = tallies.at[source_of].add(-passed).at[sink].add(passed)
    members = jnp.searchsorted(jnp.cumsum(tallies), jnp.arange(rows * top), side="right").astype(jnp.int32)
    grid = members.reshape(top, rows).T
    grid = grid[jax.random.permutation(jax.random.fold_in(own, 1), rows)]
    turn = jax.random.randint(jax.random.fold_in(own, 2), (rows, 1), 0, top)
    return jnp.take_along_axis(grid, (jnp.arange(top)[None, :] + turn) % top, axis=1)


def portions_of(number_of, total, reach, skew, full):
    portions = [(1 << 20) // math.isqrt(standing ** skew) + 1 for standing in range(1, number_of + 1)]
    largest = reach if full else min(reach, max(-(-total // number_of), total * portions[0] // sum(portions)))
    least = 1 if total - largest >= number_of - 1 else 0
    holding, spare = [largest] + [least] * (number_of - 1), total - largest - least * (number_of - 1)
    while spare > 0:
        free = [i for i in range(1, number_of) if holding[i] < largest] or [i for i in range(1, number_of) if holding[i] < reach]
        whole, remaining = sum([portions[i] for i in free]), spare
        for i in free:
            more = min(reach - holding[i], max(1, remaining * portions[i] // whole), spare)
            holding[i] = holding[i] + more
            spare = spare - more
    return np.array(holding)


def scatter_about(key, shape, spread, most, split=(), held_as=jnp.bfloat16):
    entries = spread * jax.random.normal(key, shape, jnp.float32)
    if split:
        entries = entries * shard_levels(key, shape, split, -0.22, 0.18)
    return jnp.clip(entries, -most, most).astype(held_as)


def setup_inputs(seed: int = 0, part: int = 0) -> dict:
    key_list = jax.random.split(jax.random.key(seed), 7)
    part_splits = jax.random.split(jax.random.fold_in(key_list[6], part), 7)
    lap_tiles = draw_lap_tiles(jax.random.fold_in(jax.random.fold_in(key_list[6], part), 71), part)
    tile_columns = draw_tile_columns(jax.random.fold_in(jax.random.fold_in(key_list[6], part), 71), part)
    start_block = scatter_about(part_splits[2], (V, K), 1.0, 6.0, ((0, 16),), jnp.float32)
    patch_of_keys = jax.random.split(jax.random.fold_in(part_splits[3], 1), V // V_DEV)
    patch_of_turns = jax.random.permutation(jax.random.fold_in(part_splits[3], 3), V // V_DEV)
    patch_of = jax.vmap(lambda own, number: assign_block(jax.random.fold_in(part_splits[3], 2), own, number, V_DEV, PATCHES, 1, CAP, 2))(patch_of_keys, patch_of_turns).reshape((V, 1))
    mix_weight = scatter_about(key_list[4], (2 * K, HID), (2 * K) ** -0.5, 0.5)
    class_weight = scatter_about(key_list[5], (HID, NCLS), HID ** -0.5, 0.375)
    return dict(lap_tiles=lap_tiles, tile_columns=tile_columns, start_block=start_block, patch_of=patch_of, mix_weight=mix_weight, class_weight=class_weight)


highest_precision = lax.Precision.HIGHEST

def apply_operator(vectors, lap_tiles, tile_columns):
    blocks = vectors.reshape(NB, TILE, K)

    def add_slot(total, slot_index):
        picked = blocks[tile_columns[:, slot_index]]
        coupled = lax.dynamic_index_in_dim(lap_tiles, slot_index, 1, keepdims=False)
        return (total - jnp.einsum('bij,bjk->bik', coupled, picked, precision=highest_precision), None)
    total, unused = lax.scan(add_slot, 4.0 * blocks, jnp.arange(TPB, dtype=jnp.int32))
    return total.reshape(V, K)

def cholesky_factor(vectors):
    moment = jnp.dot(vectors.T.astype(jnp.float32), vectors.astype(jnp.float32), precision=highest_precision, preferred_element_type=jnp.float32)
    return jnp.linalg.cholesky(moment)

def apply_inverse(vectors, factor):
    return jax.scipy.linalg.solve_triangular(factor, vectors.T, lower=True).T

def reference(lap_tiles, tile_columns, start_block, patch_of, mix_weight, class_weight):
    first_image = apply_operator(start_block, lap_tiles, tile_columns)
    first_basis = apply_inverse(first_image, cholesky_factor(first_image))
    second_image = apply_operator(first_basis, lap_tiles, tile_columns)
    basis = apply_inverse(second_image, cholesky_factor(second_image))
    image = apply_operator(basis, lap_tiles, tile_columns)
    ritz = jnp.dot(basis.T.astype(jnp.float32), image.astype(jnp.float32), precision=highest_precision, preferred_element_type=jnp.float32)
    scaled = math.sqrt(V) * jnp.dot(basis.astype(jnp.float32), ritz.astype(jnp.float32), precision=highest_precision, preferred_element_type=jnp.float32)
    embedding = scaled.astype(jnp.bfloat16)
    patch_ids = patch_of[:, 0]
    sums = jax.ops.segment_sum(embedding.astype(jnp.float32), patch_ids, num_segments=PATCHES)
    counts = jax.ops.segment_sum(jnp.ones((V,), jnp.float32), patch_ids, num_segments=PATCHES)
    patch_mean = (sums / counts[:, None]).astype(jnp.bfloat16)
    mean_project = jnp.dot(patch_mean.astype(jnp.float32), mix_weight[K:].astype(jnp.float32), preferred_element_type=jnp.float32)
    before = jnp.dot(embedding.astype(jnp.float32), mix_weight[:K].astype(jnp.float32), preferred_element_type=jnp.float32) + mean_project[patch_ids]
    hidden = jax.nn.gelu(before, approximate=False).astype(jnp.bfloat16)
    labels = jnp.dot(hidden.astype(jnp.float32), class_weight.astype(jnp.float32), preferred_element_type=jnp.float32).astype(jnp.bfloat16)
    return (embedding, ritz, labels)
```

```python
import functools
import math

import jax
import jax.numpy as jnp
from jax import lax
from jax.experimental import pallas as pl
from jax.experimental.pallas import tpu as pltpu
from jax.sharding import PartitionSpec as P

HALO = 2
TILE = 128
K = 64
PATCH_DEV = 4
MESH = pl.DeviceIdType.MESH
F32 = jnp.float32
BF16 = jnp.bfloat16
HIGH = lax.Precision.HIGHEST


def dot(a, b, ca=1, cb=0, precision=None):
    return lax.dot_general(
        a, b, (((ca,), (cb,)), ((), ())), precision=precision, preferred_element_type=F32
    )


def fold(x):
    return x + pltpu.roll(x, K, 1)


def low_lanes(shape):
    return lax.broadcasted_iota(jnp.int32, shape, len(shape) - 1) < K


def halves(x):
    high = x.astype(BF16)
    low = (x - high.astype(F32)).astype(BF16)
    return jnp.where(low_lanes(x.shape), high, low)


def pair_rows(x):
    high = x.astype(BF16)
    low = (x - high.astype(F32)).astype(BF16)
    return jnp.concatenate([high, low], axis=0)


def inner(left, right):
    full = dot(left, right, 0, 0)
    return fold(full[:K] + full[K:])


def inverse_factor(gram):
    lane = lax.broadcasted_iota(jnp.int32, (8, 2 * K), 1)
    sub = lax.broadcasted_iota(jnp.int32, (8, 2 * K), 0)
    slabs = []
    for s in range(K // 8):
        unit = (lane - K == sub + 8 * s).astype(F32)
        slabs.append(jnp.where(lane < K, gram[8 * s:8 * s + 8], unit))
    for k in range(K):
        s, r = divmod(k, 8)
        row = slabs[s][r:r + 1]
        scaled = row * (1.0 / row[:, k:k + 1])
        for j in range(s, K // 8):
            col = slabs[j][:, k:k + 1]
            if j == s:
                if r == 7:
                    continue
                col = jnp.where(sub[:, :1] > r, col, 0.0)
            slabs[j] = slabs[j] - col * scaled
    out = []
    for s in range(K // 8):
        diagonal = jnp.sum(jnp.where(lane == sub + 8 * s, slabs[s], 0.0), axis=1, keepdims=True)
        out.append(slabs[s] * lax.rsqrt(diagonal))
    whole = jnp.concatenate(out, axis=0)
    return jnp.where(low_lanes(whole.shape), pltpu.roll(whole, K, 1), whole)


class Summed:
    def __init__(self, n, me, off, own, recv, total, sems):
        self.n, self.me, self.off = n, me, off
        self.own, self.recv, self.total = own, recv, total
        self.sems = sems
        self.pieces = own.shape[0] // 8
        self.stride = n // self.pieces
        self.mine = lax.div(me, self.stride)
        self.owner = lax.rem(me, self.stride) == off

    def copy(self, src, dst, send, recv, device):
        return pltpu.make_async_remote_copy(
            src_ref=src, dst_ref=dst, send_sem=self.sems.at[send], recv_sem=self.sems.at[recv],
            device_id={"rows": device}, device_id_type=MESH,
        )

    def scatter(self):
        def one(p, carry):
            owner = p * self.stride + self.off
            slot = lax.rem(self.me - owner + self.n, self.n) - 1

            @pl.when(owner != self.me)
            def _():
                self.copy(
                    self.own.at[pl.ds(pl.multiple_of(p * 8, 8), 8)], self.recv.at[slot], 0, 1, owner
                ).start()
            return carry
        lax.fori_loop(0, self.pieces, one, 0, unroll=True)

    def gather(self):
        @pl.when(self.owner)
        def _():
            self.copy(self.recv, self.recv, 0, 1, self.me).wait_recv()
            part = pl.ds(pl.multiple_of(self.mine * 8, 8), 8)
            self.total[part] = self.own[part] + jnp.sum(self.recv[...], axis=0)

            def one(i, carry):
                other = lax.rem(self.me + i, self.n)
                self.copy(self.total.at[part], self.total.at[part], 2, 3, other).start()
                return carry
            lax.fori_loop(1, self.n, one, 0, unroll=self.n <= 16)

    def await_sends(self, count):
        rows = self.own.at[pl.ds(0, 8 * count)]
        self.copy(rows, rows, 0, 1, self.me).wait_send()

    def await_total(self, count):
        if count:
            rows = self.total.at[pl.ds(0, 8 * count)]
            self.copy(rows, rows, 2, 3, self.me).wait_recv()

    def finish(self):
        @pl.when(self.owner)
        def _():
            self.await_total(self.pieces - 1)
            self.await_sends(self.pieces - 1)
            self.copy(self.recv, self.recv, 2, 3, self.me).wait_send()

        @pl.when(jnp.logical_not(self.owner))
        def _():
            self.await_total(self.pieces)
            self.await_sends(self.pieces)


def kernel(
    n, lap, cols, start, ids, mix, cls,
    emb_out, ritz_out, lab_out,
    lap32, pairs, y0, y1, y2, v32, s16, w16,
    g1, g1_recv, g1_sum, g2, g2_recv, g2_sum, r3, r3_recv, r3_sum, pt, pt_recv, pt_sum,
    lap_sem, halo_send, halo_recv, g1_sem, g2_sem, r3_sem, pt_sem,
):
    blocks, slots = cols.shape
    rows = blocks * TILE
    patches = pt.shape[0]
    me = lax.axis_index("rows")
    right, left = lax.rem(me + 1, n), lax.rem(me + n - 1, n)
    def lap_copy(b):
        return pltpu.make_async_copy(lap.at[b], lap32.at[b], lap_sem.at[b])

    for b in range(blocks):
        lap_copy(b).start()

    barrier = pltpu.get_barrier_semaphore()

    def greet(i, carry):
        pl.semaphore_signal(
            barrier, inc=1, device_id={"rows": lax.rem(me + i, n)}, device_id_type=MESH
        )
        return carry
    lax.fori_loop(1, n, greet, 0)

    def halo(buf, turn):
        def one(src, dst, side, device):
            return pltpu.make_async_remote_copy(
                src_ref=buf.at[pl.ds(src, HALO)], dst_ref=buf.at[pl.ds(dst, HALO)],
                send_sem=halo_send.at[turn, side], recv_sem=halo_recv.at[turn, side],
                device_id={"rows": device}, device_id_type=MESH,
            )
        return one(blocks, 0, 0, right), one(HALO, blocks + HALO, 1, left)

    def block_rows(b):
        return pl.ds(pl.multiple_of(b * TILE, TILE), TILE)

    def stage(b, carry):
        x = start[block_rows(b), :]
        x = jnp.concatenate([x, x], axis=1)
        v32[block_rows(b), :] = x
        y0[b + HALO] = halves(x)
        return carry
    lax.fori_loop(0, blocks, stage, 0, unroll=2)
    pl.semaphore_wait(barrier, n - 1)
    for copy in halo(y0, 0):
        copy.start()

    def split(b, carry):
        lap_copy(b).wait()
        for t in range(slots):
            pairs[b, :, t * TILE:(t + 1) * TILE] = pair_rows(lap32[b, t])
        return carry
    lax.fori_loop(0, blocks, split, 0)

    def image(buf, b):
        picked = []
        for t in range(slots):
            picked.append(buf[cols[b, t]])
        product = dot(pairs[b], jnp.concatenate(picked, axis=0))
        return 4.0 * v32[block_rows(b), :] - fold(product[:TILE] + product[TILE:])

    def sweep(body, first, last):
        def one(b, carry):
            body(b)
            return carry
        lax.fori_loop(first, last, one, 0, unroll=2)

    for copy in halo(y0, 0):
        copy.wait()

    def first_step(b):
        y1[b + HALO] = halves(image(y0, b))
    sweep(first_step, 0, HALO)
    sweep(first_step, blocks - HALO, blocks)
    for copy in halo(y1, 1):
        copy.start()
    sweep(first_step, HALO, blocks - HALO)
    here = y1[HALO:HALO + blocks].reshape(rows, TILE)
    g1[...] = inner(here, here)
    sum1 = Summed(n, me, 0, g1, g1_recv, g1_sum, g1_sem)
    sum1.scatter()

    def lift(b):
        x = y1[b + HALO].astype(F32)
        v32[block_rows(b), :] = fold(x)
    sweep(lift, 0, blocks)
    for copy in halo(y1, 1):
        copy.wait()

    def second_step(b):
        s16[block_rows(b), :] = halves(image(y1, b))
    sweep(second_step, 0, blocks // 2)
    sum1.gather()
    sweep(second_step, blocks // 2, blocks)
    sum1.finish()

    w16[...] = pair_rows(inverse_factor(g1_sum[...]))

    def second_image(b):
        x = fold(dot(s16[block_rows(b), :], w16[...], 1, 1))
        v32[block_rows(b), :] = x
        y2[b + HALO] = halves(x)
    sweep(second_image, 0, HALO)
    sweep(second_image, blocks - HALO, blocks)
    for copy in halo(y2, 2):
        copy.start()
    sweep(second_image, HALO, blocks - HALO)
    here = y2[HALO:HALO + blocks].reshape(rows, TILE)
    g2[...] = inner(here, here)
    sum2 = Summed(n, me, 0, g2, g2_recv, g2_sum, g2_sem)
    sum2.scatter()

    def members(b):
        who = lax.broadcasted_iota(jnp.int32, (patches, TILE), 0)
        return (who == ids[pl.ds(b, 1), :]).astype(F32)

    def patch_step(b, carry):
        sums, counts = carry
        member = members(b)
        return (
            sums + dot(member.astype(BF16), y2[b + HALO]),
            counts + member,
        )
    zero = jnp.zeros((patches, TILE), F32)
    sums, counts = lax.fori_loop(0, blocks, patch_step, (zero, zero), unroll=2)
    counts = jnp.sum(counts, axis=1, keepdims=True)
    pt[...] = jnp.where(low_lanes((patches, TILE)), fold(sums), counts)
    sum4 = Summed(n, me, 1, pt, pt_recv, pt_sum, pt_sem)
    sum4.scatter()

    for copy in halo(y2, 2):
        copy.wait()

    def third_step(b):
        s16[block_rows(b), :] = halves(image(y2, b))
    sweep(third_step, 0, blocks // 2)
    sum2.gather()
    sweep(third_step, blocks // 2, blocks)
    r3[...] = inner(y2[HALO:HALO + blocks].reshape(rows, TILE), s16[...])
    sum3 = Summed(n, me, 0, r3, r3_recv, r3_sum, r3_sem)
    sum3.scatter()
    sum4.gather()
    sum2.finish()
    factor = inverse_factor(g2_sum[...])
    sum3.gather()
    sum4.finish()
    sum3.finish()

    narrow = factor[:, :K]
    ritz = dot(narrow, dot(r3_sum[:, :K], narrow, 1, 1, HIGH), 1, 0, HIGH)
    ritz_out[...] = ritz
    scale = math.sqrt(rows * n)
    to_embed = scale * dot(ritz, factor, 0, 0, HIGH)
    w16[...] = pair_rows(to_embed)
    gathered = pt_sum[...]
    patch_mean = dot(gathered[:, :K], to_embed[:, :K], 1, 1, HIGH) / gathered[:, K:K + 1]
    mean_project = pair_rows(dot(patch_mean.astype(BF16), mix[K:, :]))

    def head(b):
        embedding = fold(dot(y2[b + HALO], w16[...], 1, 1)).astype(BF16)[:, :K]
        emb_out[block_rows(b), :] = embedding
        member = members(b).astype(BF16)
        member = jnp.concatenate([member, member], axis=0)
        before = dot(embedding, mix[:K, :]) + dot(member, mean_project, 0, 0)
        hidden = 0.5 * before * (1.0 + lax.erf(before * math.sqrt(0.5)))
        lab_out[block_rows(b), :] = dot(hidden.astype(BF16), cls[...]).astype(BF16)
    sweep(head, 0, blocks)


def on_device(lap_tiles, tile_columns, start_block, patch_of, mix_weight, class_weight):
    n = lax.axis_size("rows")
    blocks, slots = tile_columns.shape
    rows = blocks * TILE
    patches = PATCH_DEV * n
    classes = class_weight.shape[1]
    vmem = pl.BlockSpec(memory_space=pltpu.VMEM)
    near = (tile_columns - (lax.axis_index("rows") * blocks - HALO)) % (blocks * n)

    def summed(height):
        return [
            pltpu.VMEM((height, TILE), F32),
            pltpu.VMEM((n - 1, 8, TILE), F32),
            pltpu.VMEM((height, TILE), F32),
        ]
    dma = pltpu.SemaphoreType.DMA
    padded = pltpu.VMEM((blocks + 2 * HALO, TILE, TILE), BF16)
    return pl.pallas_call(
        functools.partial(kernel, n),
        out_shape=(
            jax.ShapeDtypeStruct((rows, K), BF16),
            jax.ShapeDtypeStruct((K, K), F32),
            jax.ShapeDtypeStruct((rows, classes), BF16),
        ),
        in_specs=[
            pl.BlockSpec(memory_space=pl.ANY),
            pl.BlockSpec(memory_space=pltpu.SMEM),
            vmem, vmem, vmem, vmem,
        ],
        out_specs=(vmem, vmem, vmem),
        scratch_shapes=[
            pltpu.VMEM((blocks, slots, TILE, TILE), F32),
            pltpu.VMEM((blocks, 2 * TILE, slots * TILE), BF16),
            padded, padded, padded,
            pltpu.VMEM((rows, TILE), F32),
            pltpu.VMEM((rows, TILE), BF16),
            pltpu.VMEM((TILE, TILE), BF16),
            *summed(K), *summed(K), *summed(K), *summed(patches),
            dma((blocks,)), dma((3, 2)), dma((3, 2)),
            dma((4,)), dma((4,)), dma((4,)), dma((4,)),
        ],
        compiler_params=pltpu.CompilerParams(
            collective_id=0, has_side_effects=True, vmem_limit_bytes=48 * 1024 * 1024
        ),
    )(
        lap_tiles, near, start_block, patch_of.reshape(blocks, TILE),
        mix_weight, class_weight,
    )


def solution(mesh):
    in_specs = (
        P(("parts", "rows"), None, None, None),
        P(("parts", "rows"), None),
        P(("parts", "rows"), None),
        P(("parts", "rows"), None),
        P(),
        P(),
    )
    out_specs = (P(("parts", "rows"), None), P("parts", None), P(("parts", "rows"), None))
    return jax.shard_map(
        on_device, mesh=mesh, in_specs=in_specs, out_specs=out_specs, check_vma=False
    )
```

```python
import functools
import math

import jax
import jax.numpy as jnp
from jax import lax
from jax.experimental import pallas as pl
from jax.experimental.pallas import tpu as pltpu
from jax.sharding import PartitionSpec as P

HALO = 2
TILE = 128
K = 64
PATCH_DEV = 4
PANEL = 8
MESH = pl.DeviceIdType.MESH
F32 = jnp.float32
BF16 = jnp.bfloat16
HIGH = lax.Precision.HIGHEST


def dot(a, b, ca=1, cb=0, precision=None):
    return lax.dot_general(
        a, b, (((ca,), (cb,)), ((), ())), precision=precision, preferred_element_type=F32
    )


def fold(x):
    return x + pltpu.roll(x, K, 1)


def low_lanes(shape):
    return lax.broadcasted_iota(jnp.int32, shape, len(shape) - 1) < K


def halves(x):
    high = x.astype(BF16)
    low = (x - high.astype(F32)).astype(BF16)
    return jnp.where(low_lanes(x.shape), high, low)


def pair_rows(x):
    high = x.astype(BF16)
    low = (x - high.astype(F32)).astype(BF16)
    return jnp.concatenate([high, low], axis=0)


def inner(left, right):
    full = dot(left, right, 0, 0)
    return fold(full[:K] + full[K:])


def inverse_factor(gram):
    lane = lax.broadcasted_iota(jnp.int32, (8, 2 * K), 1)
    sub = lax.broadcasted_iota(jnp.int32, (8, 2 * K), 0)
    count = K // 8
    slabs = []
    for s in range(count):
        unit = (lane - K == sub + 8 * s).astype(F32)
        slabs.append(jnp.where(lane < K, gram[8 * s:8 * s + 8], unit))
    for k in range(0, K, PANEL):
        s, r = divmod(k, 8)
        spread = [
            [jnp.broadcast_to(slabs[j][:, k + c:k + c + 1], (8, 2 * K)) for j in range(s, count)]
            for c in range(PANEL)
        ]
        for c in range(PANEL):
            at = r + c
            over = 1.0 / spread[c][0][at:at + 1]
            column = [jnp.where(sub > at, spread[c][0], 0.0)] + spread[c][1:]
            for e in range(c + 1, PANEL):
                factor = spread[e][0][at:at + 1] * over
                spread[e] = [x - y * factor for x, y in zip(spread[e], column)]
            row = slabs[s][at:at + 1] * over
            for j in range(s, count):
                slabs[j] = slabs[j] - column[j - s] * row
    out = []
    for s in range(count):
        diagonal = jnp.sum(jnp.where(lane == sub + 8 * s, slabs[s], 0.0), axis=1, keepdims=True)
        out.append(slabs[s] * lax.rsqrt(diagonal))
    whole = jnp.concatenate(out, axis=0)
    return jnp.where(low_lanes(whole.shape), pltpu.roll(whole, K, 1), whole)


class Summed:
    def __init__(self, n, me, off, own, recv, total, sems):
        self.n, self.me, self.off = n, me, off
        self.own, self.recv, self.total = own, recv, total
        self.sems = sems
        self.pieces = own.shape[0] // 8
        self.stride = n // self.pieces
        self.mine = lax.div(me, self.stride)
        self.owner = lax.rem(me, self.stride) == off

    def copy(self, src, dst, send, recv, device):
        return pltpu.make_async_remote_copy(
            src_ref=src, dst_ref=dst, send_sem=self.sems.at[send], recv_sem=self.sems.at[recv],
            device_id={"rows": device}, device_id_type=MESH,
        )

    def scatter(self):
        def one(p, carry):
            owner = p * self.stride + self.off
            slot = lax.rem(self.me - owner + self.n, self.n) - 1

            @pl.when(owner != self.me)
            def _():
                self.copy(
                    self.own.at[pl.ds(pl.multiple_of(p * 8, 8), 8)], self.recv.at[slot], 0, 1, owner
                ).start()
            return carry
        lax.fori_loop(0, self.pieces, one, 0, unroll=True)

    def gather(self):
        @pl.when(self.owner)
        def _():
            self.copy(self.recv, self.recv, 0, 1, self.me).wait_recv()
            part = pl.ds(pl.multiple_of(self.mine * 8, 8), 8)
            self.total[part] = self.own[part] + jnp.sum(self.recv[...], axis=0)

            def one(i, carry):
                other = lax.rem(self.me + i, self.n)
                self.copy(self.total.at[part], self.total.at[part], 2, 3, other).start()
                return carry
            lax.fori_loop(1, self.n, one, 0, unroll=self.n <= 16)

    def await_sends(self, count):
        rows = self.own.at[pl.ds(0, 8 * count)]
        self.copy(rows, rows, 0, 1, self.me).wait_send()

    def await_total(self, count):
        if count:
            rows = self.total.at[pl.ds(0, 8 * count)]
            self.copy(rows, rows, 2, 3, self.me).wait_recv()

    def finish(self):
        @pl.when(self.owner)
        def _():
            self.await_total(self.pieces - 1)
            self.await_sends(self.pieces - 1)
            self.copy(self.recv, self.recv, 2, 3, self.me).wait_send()

        @pl.when(jnp.logical_not(self.owner))
        def _():
            self.await_total(self.pieces)
            self.await_sends(self.pieces)


def kernel(
    n, lap, cols, start_in, ids_in, mix_in, cls_in,
    emb_out, ritz_out, lab_out,
    start, ids, mix, cls, lap32, pairs, y0, y1, y2, v32, s16, w16,
    g1, g1_recv, g1_sum, g2, g2_recv, g2_sum, r3, r3_recv, r3_sum, pt, pt_recv, pt_sum,
    in_sem, lap_sem, halo_send, halo_recv, g1_sem, g2_sem, r3_sem, pt_sem,
):
    slots, blocks = cols.shape
    rows = blocks * TILE
    patches = pt.shape[0]
    me = lax.axis_index("rows")
    right, left = lax.rem(me + 1, n), lax.rem(me + n - 1, n)
    def lap_copy(b):
        return pltpu.make_async_copy(lap.at[b], lap32.at[b], lap_sem.at[b])

    inputs = [
        pltpu.make_async_copy(src, dst, in_sem.at[i])
        for i, (src, dst) in enumerate(
            ((start_in, start), (ids_in, ids), (mix_in, mix), (cls_in, cls)))
    ]
    for copy in inputs:
        copy.start()
    for b in range(blocks):
        lap_copy(b).start()

    barrier = pltpu.get_barrier_semaphore()

    def greet(i, carry):
        pl.semaphore_signal(
            barrier, inc=1, device_id={"rows": lax.rem(me + i, n)}, device_id_type=MESH
        )
        return carry
    lax.fori_loop(1, n, greet, 0)

    def halo(buf, turn):
        def one(src, dst, side, device):
            return pltpu.make_async_remote_copy(
                src_ref=buf.at[pl.ds(src, HALO)], dst_ref=buf.at[pl.ds(dst, HALO)],
                send_sem=halo_send.at[turn, side], recv_sem=halo_recv.at[turn, side],
                device_id={"rows": device}, device_id_type=MESH,
            )
        return one(blocks, 0, 0, right), one(HALO, blocks + HALO, 1, left)

    def block_rows(b):
        return pl.ds(pl.multiple_of(b * TILE, TILE), TILE)

    for copy in inputs:
        copy.wait()

    def stage(b, carry):
        x = start[:, block_rows(b)]
        x = jnp.concatenate([x, x], axis=0).T
        v32[block_rows(b), :] = x
        y0[b + HALO] = halves(x)
        return carry
    lax.fori_loop(0, blocks, stage, 0, unroll=2)
    pl.semaphore_wait(barrier, n - 1)
    for copy in halo(y0, 0):
        copy.start()

    def split(b, carry):
        lap_copy(b).wait()
        for t in range(slots):
            pairs[b, :, t * TILE:(t + 1) * TILE] = pair_rows(lap32[b, t])
        return carry
    lax.fori_loop(0, blocks, split, 0)

    def image(buf, b):
        picked = []
        for t in range(slots):
            picked.append(buf[cols[t, b]])
        product = dot(pairs[b], jnp.concatenate(picked, axis=0))
        return 4.0 * v32[block_rows(b), :] - fold(product[:TILE] + product[TILE:])

    def sweep(body, first, last):
        def one(b, carry):
            body(b)
            return carry
        lax.fori_loop(first, last, one, 0, unroll=min(4, last - first))

    for copy in halo(y0, 0):
        copy.wait()

    def first_step(b):
        y1[b + HALO] = halves(image(y0, b))
    sweep(first_step, 0, HALO)
    sweep(first_step, blocks - HALO, blocks)
    for copy in halo(y1, 1):
        copy.start()
    sweep(first_step, HALO, blocks - HALO)
    here = y1[HALO:HALO + blocks].reshape(rows, TILE)
    g1[...] = inner(here, here)
    sum1 = Summed(n, me, 0, g1, g1_recv, g1_sum, g1_sem)
    sum1.scatter()

    def lift(b):
        x = y1[b + HALO].astype(F32)
        v32[block_rows(b), :] = fold(x)
    sweep(lift, 0, blocks)
    for copy in halo(y1, 1):
        copy.wait()

    def second_step(b):
        s16[block_rows(b), :] = halves(image(y1, b))
    sweep(second_step, 0, blocks // 2)
    sum1.gather()
    sweep(second_step, blocks // 2, blocks)
    sum1.finish()

    w16[...] = pair_rows(inverse_factor(g1_sum[...]))

    def second_image(b):
        x = fold(dot(s16[block_rows(b), :], w16[...], 1, 1))
        v32[block_rows(b), :] = x
        y2[b + HALO] = halves(x)
    sweep(second_image, 0, HALO)
    sweep(second_image, blocks - HALO, blocks)
    for copy in halo(y2, 2):
        copy.start()
    sweep(second_image, HALO, blocks - HALO)
    here = y2[HALO:HALO + blocks].reshape(rows, TILE)
    g2[...] = inner(here, here)
    sum2 = Summed(n, me, 0, g2, g2_recv, g2_sum, g2_sem)
    sum2.scatter()

    def members(b, many=1):
        who = lax.broadcasted_iota(jnp.int32, (patches, many * TILE), 0)
        named = jnp.concatenate([ids[pl.ds(b + i, 1), :] for i in range(many)], axis=1)
        return (who == named).astype(F32)

    def patch_step(b, carry):
        sums, counts = carry
        member = members(b)
        return (
            sums + dot(member.astype(BF16), y2[b + HALO]),
            counts + member,
        )
    zero = jnp.zeros((patches, TILE), F32)
    sums, counts = lax.fori_loop(0, blocks, patch_step, (zero, zero), unroll=2)
    counts = jnp.sum(counts, axis=1, keepdims=True)
    pt[...] = jnp.where(low_lanes((patches, TILE)), fold(sums), counts)
    sum4 = Summed(n, me, 1, pt, pt_recv, pt_sum, pt_sem)
    sum4.scatter()

    for copy in halo(y2, 2):
        copy.wait()

    def third_step(b):
        s16[block_rows(b), :] = halves(image(y2, b))
    sweep(third_step, 0, blocks // 2)
    sum2.gather()
    sweep(third_step, blocks // 2, blocks)
    r3[...] = inner(y2[HALO:HALO + blocks].reshape(rows, TILE), s16[...])
    sum3 = Summed(n, me, 0, r3, r3_recv, r3_sum, r3_sem)
    sum3.scatter()
    sum4.gather()
    sum2.finish()
    factor = inverse_factor(g2_sum[...])
    sum3.gather()
    sum4.finish()
    sum3.finish()

    narrow = factor[:, :K]
    ritz = dot(narrow, dot(r3_sum[:, :K], narrow, 1, 1, HIGH), 1, 0, HIGH)
    ritz_out[...] = ritz
    scale = math.sqrt(rows * n)
    to_embed = scale * dot(ritz, factor, 0, 0, HIGH)
    w16[...] = pair_rows(to_embed)
    gathered = pt_sum[...]
    patch_mean = dot(gathered[:, :K], to_embed[:, :K], 1, 1, HIGH) / gathered[:, K:K + 1]
    mean_project = dot(mix[K:, :], patch_mean.astype(BF16), 0, 1)
    high = mean_project.astype(BF16)
    low = (mean_project - high.astype(F32)).astype(BF16)
    weights = jnp.concatenate([high, low], axis=1)
    chunk = math.gcd(blocks, 4)

    def head(c):
        at = pl.ds(pl.multiple_of(c * chunk * TILE, TILE), chunk * TILE)
        vectors = y2[pl.ds(c * chunk + HALO, chunk)].reshape(chunk * TILE, TILE)
        both = dot(w16[...], vectors, 1, 1)
        embedding = (both[:K] + both[K:]).astype(BF16)
        emb_out[:, at] = embedding
        member = members(c * chunk, chunk).astype(BF16)
        member = jnp.concatenate([member, member], axis=0)
        before = dot(mix[:K, :], embedding, 0, 0) + dot(weights, member)
        hidden = 0.5 * before * (1.0 + lax.erf(before * math.sqrt(0.5)))
        lab_out[:, at] = dot(cls[...], hidden.astype(BF16)).astype(BF16)
    sweep(head, 0, blocks // chunk)


def on_device(lap_tiles, tile_columns, start_block, patch_of, mix_weight, class_weight):
    n = lax.axis_size("rows")
    blocks, slots = tile_columns.shape
    rows = blocks * TILE
    patches = PATCH_DEV * n
    classes = class_weight.shape[1]
    vmem = pl.BlockSpec(memory_space=pltpu.VMEM)
    hbm = pl.BlockSpec(memory_space=pltpu.HBM)
    near = (tile_columns.T - (lax.axis_index("rows") * blocks - HALO)) % (blocks * n)

    def summed(height):
        return [
            pltpu.VMEM((height, TILE), F32),
            pltpu.VMEM((n - 1, 8, TILE), F32),
            pltpu.VMEM((height, TILE), F32),
        ]
    dma = pltpu.SemaphoreType.DMA
    padded = pltpu.VMEM((blocks + 2 * HALO, TILE, TILE), BF16)
    embedding, ritz, labels = pl.pallas_call(
        functools.partial(kernel, n),
        out_shape=(
            jax.ShapeDtypeStruct((K, rows), BF16),
            jax.ShapeDtypeStruct((K, K), F32),
            jax.ShapeDtypeStruct((classes, rows), BF16),
        ),
        in_specs=[
            hbm, pl.BlockSpec(memory_space=pltpu.SMEM), hbm, hbm, hbm, hbm,
        ],
        out_specs=(vmem, vmem, vmem),
        scratch_shapes=[
            pltpu.VMEM((K, rows), F32),
            pltpu.VMEM((blocks, TILE), jnp.int32),
            pltpu.VMEM(mix_weight.shape, BF16),
            pltpu.VMEM((classes, class_weight.shape[0]), BF16),
            pltpu.VMEM((blocks, slots, TILE, TILE), F32),
            pltpu.VMEM((blocks, 2 * TILE, slots * TILE), BF16),
            padded, padded, padded,
            pltpu.VMEM((rows, TILE), F32),
            pltpu.VMEM((rows, TILE), BF16),
            pltpu.VMEM((TILE, TILE), BF16),
            *summed(K), *summed(K), *summed(K), *summed(patches),
            dma((4,)), dma((blocks,)), dma((3, 2)), dma((3, 2)),
            dma((4,)), dma((4,)), dma((4,)), dma((4,)),
        ],
        compiler_params=pltpu.CompilerParams(
            collective_id=0, has_side_effects=True, vmem_limit_bytes=63 * 1024 * 1024
        ),
    )(
        lap_tiles, near, start_block.T, patch_of.reshape(blocks, TILE),
        mix_weight, class_weight.T,
    )
    return embedding.T, ritz, labels.T


def solution(mesh):
    in_specs = (
        P(("parts", "rows"), None, None, None),
        P(("parts", "rows"), None),
        P(("parts", "rows"), None),
        P(("parts", "rows"), None),
        P(),
        P(),
    )
    out_specs = (P(("parts", "rows"), None), P("parts", None), P(("parts", "rows"), None))
    return jax.shard_map(
        on_device, mesh=mesh, in_specs=in_specs, out_specs=out_specs, check_vma=False
    )
```

```python
import functools
import math

import jax
import jax.numpy as jnp
from jax import lax
from jax.experimental import pallas as pl
from jax.experimental.pallas import tpu as pltpu
from jax.sharding import PartitionSpec as P

HALO = 2
TILE = 128
K = 64
PATCH_DEV = 4
PANEL = 8
MESH = pl.DeviceIdType.MESH
F32 = jnp.float32
BF16 = jnp.bfloat16
HIGH = lax.Precision.HIGHEST


def dot(a, b, ca=1, cb=0, precision=None):
    return lax.dot_general(
        a, b, (((ca,), (cb,)), ((), ())), precision=precision, preferred_element_type=F32
    )


def fold(x):
    return x + pltpu.roll(x, K, 1)


def low_lanes(shape):
    return lax.broadcasted_iota(jnp.int32, shape, len(shape) - 1) < K


def halves(x):
    high = x.astype(BF16)
    low = (x - high.astype(F32)).astype(BF16)
    return jnp.where(low_lanes(x.shape), high, low)


def pair_rows(x):
    high = x.astype(BF16)
    low = (x - high.astype(F32)).astype(BF16)
    return jnp.concatenate([high, low], axis=0)


def inner(left, right):
    full = dot(left, right, 0, 0)
    return fold(full[:K] + full[K:])


def inverse_factor(gram):
    lane = lax.broadcasted_iota(jnp.int32, (8, 2 * K), 1)
    sub = lax.broadcasted_iota(jnp.int32, (8, 2 * K), 0)
    count = K // 8
    slabs = []
    for s in range(count):
        unit = (lane - K == sub + 8 * s).astype(F32)
        slabs.append(jnp.where(lane < K, gram[8 * s:8 * s + 8], unit))
    for k in range(0, K, PANEL):
        s, r = divmod(k, 8)
        spread = [
            [jnp.broadcast_to(slabs[j][:, k + c:k + c + 1], (8, 2 * K)) for j in range(s, count)]
            for c in range(PANEL)
        ]
        for c in range(PANEL):
            at = r + c
            over = 1.0 / spread[c][0][at:at + 1]
            column = [jnp.where(sub > at, spread[c][0], 0.0)] + spread[c][1:]
            for e in range(c + 1, PANEL):
                factor = spread[e][0][at:at + 1] * over
                spread[e] = [x - y * factor for x, y in zip(spread[e], column)]
            row = slabs[s][at:at + 1] * over
            for j in range(s, count):
                slabs[j] = slabs[j] - column[j - s] * row
    out = []
    for s in range(count):
        diagonal = jnp.sum(jnp.where(lane == sub + 8 * s, slabs[s], 0.0), axis=1, keepdims=True)
        out.append(slabs[s] * lax.rsqrt(diagonal))
    whole = jnp.concatenate(out, axis=0)
    return jnp.where(low_lanes(whole.shape), pltpu.roll(whole, K, 1), whole)


class Summed:
    def __init__(self, n, me, off, own, recv, total, sems):
        self.n, self.me, self.off = n, me, off
        self.own, self.recv, self.total = own, recv, total
        self.sems = sems
        self.pieces = own.shape[0] // 8
        self.stride = n // self.pieces
        self.mine = lax.div(me, self.stride)
        self.owner = lax.rem(me, self.stride) == off

    def copy(self, src, dst, send, recv, device):
        return pltpu.make_async_remote_copy(
            src_ref=src, dst_ref=dst, send_sem=self.sems.at[send], recv_sem=self.sems.at[recv],
            device_id={"rows": device}, device_id_type=MESH,
        )

    def scatter(self):
        def one(p, carry):
            owner = p * self.stride + self.off
            slot = lax.rem(self.me - owner + self.n, self.n) - 1

            @pl.when(owner != self.me)
            def _():
                self.copy(
                    self.own.at[pl.ds(pl.multiple_of(p * 8, 8), 8)], self.recv.at[slot], 0, 1, owner
                ).start()
            return carry
        lax.fori_loop(0, self.pieces, one, 0, unroll=True)

    def gather(self):
        @pl.when(self.owner)
        def _():
            self.copy(self.recv, self.recv, 0, 1, self.me).wait_recv()
            part = pl.ds(pl.multiple_of(self.mine * 8, 8), 8)
            self.total[part] = self.own[part] + jnp.sum(self.recv[...], axis=0)

            def one(i, carry):
                other = lax.rem(self.me + i, self.n)
                self.copy(self.total.at[part], self.total.at[part], 2, 3, other).start()
                return carry
            lax.fori_loop(1, self.n, one, 0, unroll=self.n <= 16)

    def await_sends(self, count):
        rows = self.own.at[pl.ds(0, 8 * count)]
        self.copy(rows, rows, 0, 1, self.me).wait_send()

    def await_total(self, count):
        if count:
            rows = self.total.at[pl.ds(0, 8 * count)]
            self.copy(rows, rows, 2, 3, self.me).wait_recv()

    def finish(self):
        @pl.when(self.owner)
        def _():
            self.await_total(self.pieces - 1)
            self.await_sends(self.pieces - 1)
            self.copy(self.recv, self.recv, 2, 3, self.me).wait_send()

        @pl.when(jnp.logical_not(self.owner))
        def _():
            self.await_total(self.pieces)
            self.await_sends(self.pieces)


def kernel(
    n, lap, cols, start_in, ids_in, mix_in,
    image_out, ritz_out, factor_out, mean_out,
    start, ids, mix, lap32, pairs, y0, y1, y2, v32, s16, w16,
    g1, g1_recv, g1_sum, g2, g2_recv, g2_sum, r3, r3_recv, r3_sum, pt, pt_recv, pt_sum,
    in_sem, lap_sem, halo_send, halo_recv, g1_sem, g2_sem, r3_sem, pt_sem,
):
    slots, blocks = cols.shape
    rows = blocks * TILE
    patches = pt.shape[0]
    me = lax.axis_index("rows")
    right, left = lax.rem(me + 1, n), lax.rem(me + n - 1, n)
    def lap_copy(b):
        return pltpu.make_async_copy(lap.at[b], lap32.at[b], lap_sem.at[b])

    inputs = [
        pltpu.make_async_copy(src, dst, in_sem.at[i])
        for i, (src, dst) in enumerate(
            ((start_in, start), (ids_in, ids), (mix_in, mix)))
    ]
    for copy in inputs:
        copy.start()
    for b in range(blocks):
        lap_copy(b).start()

    barrier = pltpu.get_barrier_semaphore()

    def greet(i, carry):
        pl.semaphore_signal(
            barrier, inc=1, device_id={"rows": lax.rem(me + i, n)}, device_id_type=MESH
        )
        return carry
    lax.fori_loop(1, n, greet, 0, unroll=n <= 16)

    def halo(buf, turn):
        def one(src, dst, side, device):
            return pltpu.make_async_remote_copy(
                src_ref=buf.at[pl.ds(src, HALO)], dst_ref=buf.at[pl.ds(dst, HALO)],
                send_sem=halo_send.at[turn, side], recv_sem=halo_recv.at[turn, side],
                device_id={"rows": device}, device_id_type=MESH,
            )
        return one(blocks, 0, 0, right), one(HALO, blocks + HALO, 1, left)

    def block_rows(b):
        return pl.ds(pl.multiple_of(b * TILE, TILE), TILE)

    for copy in inputs:
        copy.wait()

    def stage(b, carry):
        x = start[:, block_rows(b)]
        x = jnp.concatenate([x, x], axis=0).T
        v32[block_rows(b), :] = x
        y0[b + HALO] = halves(x)
        return carry
    lax.fori_loop(0, blocks, stage, 0, unroll=2)
    pl.semaphore_wait(barrier, n - 1)
    for copy in halo(y0, 0):
        copy.start()

    def split(b, carry):
        lap_copy(b).wait()
        for t in range(slots):
            pairs[b, :, t * TILE:(t + 1) * TILE] = pair_rows(lap32[b, t])
        return carry
    lax.fori_loop(0, blocks, split, 0)

    def near(column):
        whole = blocks * n
        at = column - me * blocks + HALO
        at = at & (whole - 1) if whole & (whole - 1) == 0 else lax.rem(at + whole, whole)
        return jnp.minimum(at, blocks + 2 * HALO - 1)

    def image(buf, b):
        picked = []
        for t in range(slots):
            picked.append(buf[near(cols[t, b])])
        product = dot(pairs[b], jnp.concatenate(picked, axis=0))
        return 4.0 * v32[block_rows(b), :] - fold(product[:TILE] + product[TILE:])

    def sweep(body, first, last):
        def one(b, carry):
            body(b)
            return carry
        lax.fori_loop(first, last, one, 0, unroll=min(4, last - first))

    for copy in halo(y0, 0):
        copy.wait()

    def first_step(b):
        y1[b + HALO] = halves(image(y0, b))
    sweep(first_step, 0, HALO)
    sweep(first_step, blocks - HALO, blocks)
    for copy in halo(y1, 1):
        copy.start()
    sweep(first_step, HALO, blocks - HALO)
    here = y1[HALO:HALO + blocks].reshape(rows, TILE)
    g1[...] = inner(here, here)
    sum1 = Summed(n, me, 0, g1, g1_recv, g1_sum, g1_sem)
    sum1.scatter()

    def lift(b):
        x = y1[b + HALO].astype(F32)
        v32[block_rows(b), :] = fold(x)
    sweep(lift, 0, blocks)
    for copy in halo(y1, 1):
        copy.wait()

    def second_step(b):
        s16[block_rows(b), :] = halves(image(y1, b))
    sweep(second_step, 0, blocks // 2)
    sum1.gather()
    sweep(second_step, blocks // 2, blocks)
    sum1.finish()

    w16[...] = pair_rows(inverse_factor(g1_sum[...]))

    def second_image(b):
        x = fold(dot(s16[block_rows(b), :], w16[...], 1, 1))
        v32[block_rows(b), :] = x
        y2[b + HALO] = halves(x)
    sweep(second_image, 0, HALO)
    sweep(second_image, blocks - HALO, blocks)
    for copy in halo(y2, 2):
        copy.start()
    sweep(second_image, HALO, blocks - HALO)
    kept = pltpu.make_async_copy(y2.at[pl.ds(HALO, blocks)], image_out, in_sem.at[3])
    kept.start()
    here = y2[HALO:HALO + blocks].reshape(rows, TILE)
    g2[...] = inner(here, here)
    sum2 = Summed(n, me, 0, g2, g2_recv, g2_sum, g2_sem)
    sum2.scatter()

    def members(b):
        who = lax.broadcasted_iota(jnp.int32, (patches, TILE), 0)
        return (who == ids[pl.ds(b, 1), :]).astype(F32)

    def patch_step(b, carry):
        sums, counts = carry
        member = members(b)
        return (
            sums + dot(member.astype(BF16), y2[b + HALO]),
            counts + member,
        )
    zero = jnp.zeros((patches, TILE), F32)
    sums, counts = lax.fori_loop(0, blocks, patch_step, (zero, zero), unroll=2)
    counts = jnp.sum(counts, axis=1, keepdims=True)
    pt[...] = jnp.where(low_lanes((patches, TILE)), fold(sums), counts)
    sum4 = Summed(n, me, 1, pt, pt_recv, pt_sum, pt_sem)
    sum4.scatter()

    for copy in halo(y2, 2):
        copy.wait()

    def third_step(b):
        s16[block_rows(b), :] = halves(image(y2, b))
    sweep(third_step, 0, blocks // 2)
    sum2.gather()
    sum4.gather()
    sweep(third_step, blocks // 2, blocks)
    r3[...] = inner(y2[HALO:HALO + blocks].reshape(rows, TILE), s16[...])
    sum3 = Summed(n, me, 0, r3, r3_recv, r3_sum, r3_sem)
    sum3.scatter()
    sum2.finish()
    factor = inverse_factor(g2_sum[...])
    sum3.gather()
    sum4.finish()
    sum3.finish()

    narrow = factor[:, :K]
    ritz = dot(narrow, dot(r3_sum[:, :K], narrow, 1, 1, HIGH), 1, 0, HIGH)
    ritz_out[...] = ritz
    scale = math.sqrt(rows * n)
    to_embed = scale * dot(ritz, factor, 0, 0, HIGH)
    factor_out[...] = pair_rows(to_embed)
    gathered = pt_sum[...]
    patch_mean = dot(gathered[:, :K], to_embed[:, :K], 1, 1, HIGH) / gathered[:, K:K + 1]
    mean_project = dot(mix[K:, :], patch_mean.astype(BF16), 0, 1)
    high = mean_project.astype(BF16)
    low = (mean_project - high.astype(F32)).astype(BF16)
    mean_out[...] = jnp.concatenate([high, low], axis=1)
    kept.wait()


def head(image, ritz, factor, mean, ids, mix, cls, emb_out, ritz_out, lab_out):
    ritz_out[...] = ritz[...]
    chunk = image.shape[0]
    patches = mean.shape[1] // 2
    both = dot(factor[...], image[...].reshape(chunk * TILE, TILE), 1, 1)
    embedding = (both[:K] + both[K:]).astype(BF16)
    emb_out[...] = embedding
    who = lax.broadcasted_iota(jnp.int32, (patches, chunk * TILE), 0)
    first = pl.program_id(0) * chunk
    named = jnp.concatenate([ids[pl.ds(first + i, 1), :] for i in range(chunk)], axis=1)
    member = (who == named).astype(F32).astype(BF16)
    member = jnp.concatenate([member, member], axis=0)
    before = dot(mix[:K, :], embedding, 0, 0) + dot(mean[...], member)
    hidden = 0.5 * before * (1.0 + lax.erf(before * math.sqrt(0.5)))
    lab_out[...] = dot(cls[...], hidden.astype(BF16)).astype(BF16)


def on_device(lap_tiles, tile_columns, start_block, patch_of, mix_weight, class_weight):
    n = lax.axis_size("rows")
    blocks, slots = tile_columns.shape
    rows = blocks * TILE
    patches = PATCH_DEV * n
    classes = class_weight.shape[1]
    vmem = pl.BlockSpec(memory_space=pltpu.VMEM)
    hbm = pl.BlockSpec(memory_space=pltpu.HBM)
    columns = tile_columns.T

    def summed(height):
        return [
            pltpu.VMEM((height, TILE), F32),
            pltpu.VMEM((n - 1, 8, TILE), F32),
            pltpu.VMEM((height, TILE), F32),
        ]
    dma = pltpu.SemaphoreType.DMA
    padded = pltpu.VMEM((blocks + 2 * HALO, TILE, TILE), BF16)
    named = patch_of.reshape(blocks, TILE)
    hidden = mix_weight.shape[1]
    image, ritz, factor, mean = pl.pallas_call(
        functools.partial(kernel, n),
        out_shape=(
            jax.ShapeDtypeStruct((blocks, TILE, TILE), BF16),
            jax.ShapeDtypeStruct((K, K), F32),
            jax.ShapeDtypeStruct((TILE, TILE), BF16),
            jax.ShapeDtypeStruct((hidden, 2 * patches), BF16),
        ),
        in_specs=[
            hbm, pl.BlockSpec(memory_space=pltpu.SMEM), hbm, hbm, hbm,
        ],
        out_specs=(hbm, vmem, vmem, vmem),
        scratch_shapes=[
            pltpu.VMEM((K, rows), F32),
            pltpu.VMEM((blocks, TILE), jnp.int32),
            pltpu.VMEM(mix_weight.shape, BF16),
            pltpu.VMEM((blocks, slots, TILE, TILE), F32),
            pltpu.VMEM((blocks, 2 * TILE, slots * TILE), BF16),
            padded, padded, padded,
            pltpu.VMEM((rows, TILE), F32),
            pltpu.VMEM((rows, TILE), BF16),
            pltpu.VMEM((TILE, TILE), BF16),
            *summed(K), *summed(K), *summed(K), *summed(patches),
            dma((4,)), dma((blocks,)), dma((3, 2)), dma((3, 2)),
            dma((4,)), dma((4,)), dma((4,)), dma((4,)),
        ],
        compiler_params=pltpu.CompilerParams(
            collective_id=0, has_side_effects=True, vmem_limit_bytes=63 * 1024 * 1024
        ),
    )(
        lap_tiles, columns, start_block.T, named, mix_weight,
    )
    chunk = math.gcd(blocks, 4)

    def fixed(shape):
        return pl.BlockSpec(shape, lambda c: (0, 0))

    embedding, ritz, labels = pl.pallas_call(
        head,
        grid=(blocks // chunk,),
        out_shape=(
            jax.ShapeDtypeStruct((K, rows), BF16),
            jax.ShapeDtypeStruct((K, K), F32),
            jax.ShapeDtypeStruct((classes, rows), BF16),
        ),
        in_specs=[
            pl.BlockSpec((chunk, TILE, TILE), lambda c: (c, 0, 0)),
            fixed((K, K)), fixed((TILE, TILE)), fixed((hidden, 2 * patches)),
            fixed((blocks, TILE)), fixed((2 * K, hidden)), fixed((classes, hidden)),
        ],
        out_specs=(
            pl.BlockSpec((K, chunk * TILE), lambda c: (0, c)),
            fixed((K, K)),
            pl.BlockSpec((classes, chunk * TILE), lambda c: (0, c)),
        ),
        compiler_params=pltpu.CompilerParams(vmem_limit_bytes=63 * 1024 * 1024),
    )(image, ritz, factor, mean, named, mix_weight, class_weight.T)
    return embedding.T, ritz, labels.T


def solution(mesh):
    in_specs = (
        P(("parts", "rows"), None, None, None),
        P(("parts", "rows"), None),
        P(("parts", "rows"), None),
        P(("parts", "rows"), None),
        P(),
        P(),
    )
    out_specs = (P(("parts", "rows"), None), P("parts", None), P(("parts", "rows"), None))
    return jax.shard_map(
        on_device, mesh=mesh, in_specs=in_specs, out_specs=out_specs, check_vma=False
    )
```
